32 devices in a mesh: shard: 8 (over y, x, core), rep: 4 (over z).
Axes of the slice: x: 2, y: 2, z: 4, core: 2. Of those that a mesh axis runs over, the one named last changes fastest.
Arguments:
- docs: bfloat16 [4096, 16384], P('shard', 'rep')
- pattern: int32 [32, 128], P('shard', 'rep'), may hold values 0 or 1
- owners: int32 [4], replicated, may hold values from 0 to 7
Outputs:
- scores: bfloat16 [4, 256, 4096], P(None, ('shard', 'rep'))
The draws below stay inside these ranges and needn't reach their ends.
All inputs are finite; a program needn't handle non-finite values. No bound on the sum of `pattern` on one device may be relied on, other than what follows from the above.
Results may differ from the reference program's by a relative error of at most 0.001.
Values may be sent and summed in bfloat16 or wider, within the bound.
A program may use at most 128 MiB of HBM per device.

```python
import math
import jax
import jax.numpy as jnp
from jax import lax

TILE = 128
TERMS = 16384
DOC_DEV = 512
QUERY = 256
STEPS = 4
TILES = 128
DOCS = 4096
N_SHARD = 8


def draw_docs(key, part):
    first_key, second_key, third_key = jax.random.split(jax.random.fold_in(key, 17), 3)
    base = jnp.clip(jax.random.normal(first_key, (DOCS, TERMS), jnp.float32), -6.0, 6.0)
    row_scale = jnp.exp(jax.random.uniform(second_key, (DOCS, 1), jnp.float32) * math.log(10.0))
    column_scale = jnp.exp(jax.random.uniform(third_key, (1, TERMS), jnp.float32) * math.log(10.0))
    return (base * row_scale * column_scale).astype(jnp.bfloat16)


def plant(array, own_key, least, high):
    longest = array.shape.index(max(array.shape))
    spots = []
    for shift in (0, 1):
        where = [jax.random.randint(jax.random.fold_in(own_key, axis), (), 0, length) for axis, length in enumerate(array.shape)]
        where[longest] = (where[longest] + shift) % array.shape[longest]
        spots.append(tuple(where))
    return array.at[spots[0]].set(least).at[spots[1]].set(high)


def setup_inputs(seed: int = 0) -> dict:
    key_list = jax.random.split(jax.random.key(seed), 4)
    docs = draw_docs(jax.random.fold_in(key_list[3], 71), 0)
    pattern = plant((jax.random.randint(key_list[1], (DOCS // TILE, TILES), 0, 2) < 1).astype(jnp.int32), jax.random.fold_in(key_list[1], 1), 0, 1)
    owners = plant(jax.random.randint(key_list[2], (STEPS,), 0, N_SHARD), jax.random.fold_in(key_list[2], 1), 0, N_SHARD - 1).astype(jnp.int32)
    return {"docs": docs, "pattern": pattern, "owners": owners}


EPSILON = 1e-06
CLIP_LEVEL = 1.5

def reference(docs, pattern, owners):
    weights = pattern.astype(jnp.bfloat16)
    masked = (docs.reshape(DOCS // TILE, TILE, TILES, TILE) * weights[:, None, :, None]).reshape(DOCS, TERMS)
    by_shard = masked.reshape(N_SHARD, DOC_DEV, TERMS)

    def square_sums(block_rows):
        values = block_rows.astype(jnp.float32)
        return lax.optimization_barrier(jnp.sum(values * values, axis=1))
    doc_sq = lax.map(square_sums, by_shard).reshape(DOCS)
    inverse = lax.rsqrt(doc_sq + EPSILON)
    sharpen = math.sqrt(TERMS) * 0.5
    results = []
    for step_index in range(STEPS):
        offset = step_index % (DOC_DEV // QUERY) * QUERY
        first_row = (owners[step_index] * DOC_DEV + offset).astype(jnp.int32)
        queries = lax.dynamic_slice_in_dim(masked, first_row, QUERY, 0)
        query_inv = lax.dynamic_slice_in_dim(inverse, first_row, QUERY, 0)

        def products(block_rows):
            return lax.dot_general(queries, block_rows, (((1,), (1,)), ((), ())), preferred_element_type=jnp.float32)
        similar = lax.map(products, by_shard).transpose(1, 0, 2).reshape(QUERY, DOCS)
        scaled = similar * query_inv[:, None] * inverse[None, :] * sharpen
        results.append(jnp.clip(scaled, -CLIP_LEVEL, CLIP_LEVEL).astype(jnp.bfloat16))
    return jnp.stack(results)
```

```python
import math

import jax
import jax.numpy as jnp
from jax import lax
from jax.experimental import pallas as pl
from jax.experimental.pallas import tpu as pltpu
from jax.sharding import PartitionSpec as P

TERMS = 16384
QUERY = 256
STEPS = 4
EDGE = 128


EPSILON = 1e-06
CLIP_LEVEL = 1.5
SHARPEN = math.sqrt(TERMS) * 0.5

CHIPS = 4
REPS = 4
CHUNK = 256
GROUPS = ((0, 1), (2, 3))
MESH = pl.DeviceIdType.MESH


def ring(index):
    return index + (index // 2) * (1 - 2 * (index % 2))


def joined(
    owners, pattern, docs, out,
    mine, cross, stage, arrived, partial, sibling, summed, others, norm_parts, inverse, query_column, held, final, landed,
    cross_send, cross_recv, ring_send, ring_recv, core_send, core_recv, rep_send, rep_recv,
    norm_send, norm_recv, inv_send, inv_recv, out_send, out_recv,
):
    shard = lax.axis_index("shard")
    rep = lax.axis_index("rep")
    core = shard % 2
    chip = shard // 2
    place = ring(chip)
    mate = chip * 2 + 1 - core
    onward = ring((place + 1 + 2 * core) % CHIPS) * 2 + core
    chunks = mine.shape[0]
    rows = docs.shape[0]
    shards = 2 * CHIPS

    barrier = pltpu.get_barrier_semaphore()
    for d in range(1, shards):
        pl.semaphore_signal(barrier, inc=1, device_id=((shard + d) % shards, rep), device_id_type=MESH)
    for d in range(1, REPS):
        pl.semaphore_signal(barrier, inc=1, device_id=(shard, (rep + d) % REPS), device_id_type=MESH)
    pl.semaphore_wait(barrier, shards - 1 + REPS - 1)

    def copy(src, dst, send, recv, to):
        return pltpu.make_async_remote_copy(
            src_ref=src, dst_ref=dst, send_sem=send, recv_sem=recv, device_id=to, device_id_type=MESH
        )

    def cross_copy(k):
        return copy(cross.at[k], mine.at[k, core], cross_send.at[k], cross_recv.at[k], (mate, rep))

    def masked_chunk(half, k):
        index = half * chunks + k
        parts = []
        for i in range(rows // EDGE):
            cols = []
            for j in range(CHUNK // EDGE):
                weight = pattern[i, index * (CHUNK // EDGE) + j].astype(jnp.float32)
                block = docs[i * EDGE : (i + 1) * EDGE, pl.ds(pl.multiple_of(index * CHUNK + j * EDGE, EDGE), EDGE)]
                cols.append(block * jnp.full((EDGE, EDGE), weight, jnp.float32).astype(jnp.bfloat16))
            parts.append(cols)
        return parts

    def put(ref, k, lead, parts, squares):
        added = []
        for i, cols in enumerate(parts):
            total = None
            for j, block in enumerate(cols):
                at = (slice(i * EDGE, (i + 1) * EDGE), slice(j * EDGE, (j + 1) * EDGE))
                ref[(k, *lead, *at)] = block
                wide = block.astype(jnp.float32)
                total = wide * wide if total is None else total + wide * wide
            added.append(total)
        return squares + jnp.concatenate(added, axis=0)

    def to_mate(k, squares):
        squares = put(cross, k, (), masked_chunk(1 - core, k), squares)
        cross_copy(k).start()
        return squares

    def to_self(k, squares):
        return put(mine, k, (core,), masked_chunk(core, k), squares)

    squares = lax.fori_loop(0, chunks, to_mate, jnp.zeros((rows, EDGE), jnp.float32))
    squares = lax.fori_loop(0, chunks, to_self, squares)

    def as_row(column):
        return jnp.transpose(jnp.broadcast_to(column, (column.shape[0], 128)))[:8]

    norm_parts[0] = as_row(jnp.sum(squares, axis=1, keepdims=True))

    def norm_copy(d):
        return copy(norm_parts.at[0], norm_parts.at[d], norm_send.at[d], norm_recv.at[d], (shard, (rep + d) % REPS))

    for d in range(1, REPS):
        norm_copy(d).start()

    for k in range(chunks):
        cross_copy(k).wait_recv()

    def inv_copy(d):
        return copy(
            inverse.at[shard], inverse.at[shard], inv_send.at[d], inv_recv.at[d], ((shard + d) % shards, rep)
        )

    def inv_arrival(d):
        slot = inverse.at[(shard + shards - d) % shards]
        return copy(slot, slot, inv_send.at[d], inv_recv.at[d], ((shard + d) % shards, rep))

    def norms():
        for d in range(1, REPS):
            norm_copy(d).wait_recv()
        inverse[shard] = lax.rsqrt(norm_parts[0] + norm_parts[1] + norm_parts[2] + norm_parts[3] + EPSILON)
        for d in range(1, shards):
            inv_copy(d).start()

    def ring_copy(s, t):
        return copy(stage.at[s, t], arrived.at[s, t], ring_send.at[s, t], ring_recv.at[s, t], (onward, rep))

    def core_copy(s):
        return copy(partial.at[s, :, 1 - core], sibling.at[s], core_send.at[s], core_recv.at[s], (mate, rep))

    def rep_copy(s, d):
        to = (rep + d) % REPS
        return copy(summed.at[s, :, to], others.at[s, d - 1], rep_send.at[s, d - 1], rep_recv.at[s, d - 1], (shard, to))

    def out_copy(g, d):
        to = (chip + d) % CHIPS
        lines = pl.ds(g * 16, 16)
        return copy(
            final.at[to, lines], landed.at[chip, lines], out_send.at[g, d - 1], out_recv.at[g, d - 1],
            (to * 2 + core, rep),
        )

    def out_arrival(g, d):
        lines = pl.ds(g * 16, 16)
        slot = landed.at[(chip + CHIPS - d) % CHIPS, lines]
        return copy(slot, slot, out_send.at[g, d - 1], out_recv.at[g, d - 1], (((chip + d) % CHIPS) * 2 + core, rep))

    def to_sibling(g):
        for s in GROUPS[g]:
            core_copy(s).start()

    def to_reps(g):
        for s in GROUPS[g]:
            core_copy(s).wait_recv()
            summed[s] = partial[s, :, core] + sibling[s]
            for d in (2, 1, 3):
                rep_copy(s, d).start()

    def finish(g):
        columns = jnp.concatenate([inverse[2 * chip, 0:1, :], inverse[2 * chip + 1, 0:1, :]], axis=1)
        for s in GROUPS[g]:
            offset = s % (rows // QUERY) * QUERY
            line = inverse[owners[s], 0:1, offset : offset + QUERY]
            query_column[...] = jnp.transpose(jnp.broadcast_to(line, (128, QUERY)))
            for d in range(1, REPS):
                rep_copy(s, d).wait_recv()
            for to in range(CHIPS):
                first = pl.multiple_of((to * 2 + core) * 32 + rep * 8, 8)
                total = summed[s, to, rep] + others[s, 0, to] + others[s, 1, to] + others[s, 2, to]
                query_inv = query_column[pl.ds(first, 8), 0:1]
                scaled = total * query_inv * columns * SHARPEN
                held[s % 2, to] = jnp.clip(scaled, -CLIP_LEVEL, CLIP_LEVEL)
        for to in range(CHIPS):
            final[to, g * 16 : (g + 1) * 16, :] = jnp.concatenate([held[0, to], held[1, to]], axis=0).astype(jnp.bfloat16)
        for d in range(1, CHIPS):
            out_copy(g, d).start()

    for g, steps in enumerate(GROUPS):
        for s in steps:
            partial[s] = jnp.zeros(partial.shape[1:], jnp.float32)

        def body(t, carry, g=g, steps=steps):
            here = jnp.minimum(t, chunks - 1)
            for s in steps:
                half = s % (rows // QUERY) * QUERY
                first = mine[here, 0, half : half + QUERY, :]
                second = mine[here, 1, half : half + QUERY, :]
                own = jnp.where(owners[s] % 2 == 0, first, second)
                own = jnp.where(t < chunks, own, jnp.zeros_like(own))
                is_own = owners[s] // 2 == chip

                @pl.when(t == 0)
                def _():
                    stage[s, t] = jnp.where(is_own, own, jnp.zeros_like(own))

                @pl.when(t > 0)
                def _():
                    ring_copy(s, t - 1).wait_recv()
                    stage[s, t] = jnp.where(is_own, own, arrived[s, t - 1])

                @pl.when(t < chunks + 2)
                def _():
                    ring_copy(s, t).start()

            if g == 0:
                @pl.when(t == 1)
                def _():
                    norms()
            else:
                @pl.when(t == 2)
                def _():
                    to_reps(g - 1)

                @pl.when(t == chunks + 1)
                def _():
                    finish(g - 1)

            for s in steps:
                away = place + CHIPS - ring(owners[s] // 2)
                away = jnp.where(core == 0, away, 2 * CHIPS - away) % CHIPS
                index = jnp.clip(t - away, 0, chunks - 1)
                block = mine[index].reshape(2 * rows, CHUNK)
                product = lax.dot_general(
                    stage[s, t], block, (((1,), (1,)), ((), ())), preferred_element_type=jnp.float32
                )
                partial[s] += product.reshape(partial.shape[1:])
            return carry

        lax.fori_loop(0, chunks + 3, body, 0)
        if g == 0:
            for d in range(1, shards):
                inv_arrival(d).wait_recv()
        to_sibling(g)

    last = len(GROUPS) - 1
    to_reps(last)
    finish(last)
    for g in range(len(GROUPS)):
        landed[chip, g * 16 : (g + 1) * 16, :] = final[chip, g * 16 : (g + 1) * 16, :]
    for g in range(len(GROUPS)):
        for d in range(1, CHIPS):
            out_arrival(g, d).wait_recv()
    for c in range(CHIPS):
        out[:, c * 2 * rows : (c + 1) * 2 * rows] = landed[c]

    for k in range(chunks):
        cross_copy(k).wait_send()
    for d in range(1, REPS):
        norm_copy(d).wait_send()
    for d in range(1, shards):
        inv_copy(d).wait_send()
    for s in range(STEPS):
        lax.fori_loop(0, chunks + 2, lambda t, c, s=s: (ring_copy(s, t).wait_send(), c)[1], 0)
        core_copy(s).wait_send()
        for d in range(1, REPS):
            rep_copy(s, d).wait_send()
    for g in range(len(GROUPS)):
        for d in range(1, CHIPS):
            out_copy(g, d).wait_send()


def on_ring(docs, pattern, owners):
    rows, terms = docs.shape
    chunks = terms // 2 // CHUNK
    bf16, f32 = jnp.bfloat16, jnp.float32
    dma = pltpu.SemaphoreType.DMA
    slots = chunks + 2
    lines = STEPS * 8
    buffers = [
        pltpu.VMEM((chunks, 2, rows, CHUNK), bf16),
        pltpu.VMEM((chunks, rows, CHUNK), bf16),
        pltpu.VMEM((STEPS, slots + 1, QUERY, CHUNK), bf16),
        pltpu.VMEM((STEPS, slots, QUERY, CHUNK), bf16),
        pltpu.VMEM((STEPS, CHIPS, 2, REPS, 8, 2 * rows), f32),
        pltpu.VMEM((STEPS, CHIPS, REPS, 8, 2 * rows), f32),
        pltpu.VMEM((STEPS, CHIPS, REPS, 8, 2 * rows), f32),
        pltpu.VMEM((STEPS, REPS - 1, CHIPS, 8, 2 * rows), f32),
        pltpu.VMEM((REPS, 8, rows), f32),
        pltpu.VMEM((2 * CHIPS, 8, rows), f32),
        pltpu.VMEM((QUERY, 128), f32),
        pltpu.VMEM((2, CHIPS, 8, 2 * rows), f32),
        pltpu.VMEM((CHIPS, lines, 2 * rows), bf16),
        pltpu.VMEM((CHIPS, lines, 2 * rows), bf16),
    ]
    semaphores = []
    for shape in (
        (chunks,), (STEPS, slots), (STEPS,), (STEPS, REPS - 1), (REPS,), (2 * CHIPS,), (len(GROUPS), CHIPS - 1)
    ):
        semaphores += [dma(shape), dma(shape)]
    flops = 2 * STEPS * QUERY * rows * terms
    return pl.pallas_call(
        joined,
        out_shape=jax.ShapeDtypeStruct((lines, 2 * CHIPS * rows), bf16),
        in_specs=[
            pl.BlockSpec(memory_space=pltpu.SMEM),
            pl.BlockSpec(memory_space=pltpu.SMEM),
            pl.BlockSpec(memory_space=pltpu.VMEM),
        ],
        out_specs=pl.BlockSpec(memory_space=pltpu.VMEM),
        scratch_shapes=buffers + semaphores,
        cost_estimate=pl.CostEstimate(flops=flops, bytes_accessed=rows * terms * 2, transcendentals=0),
        compiler_params=pltpu.CompilerParams(
            collective_id=0, has_side_effects=True, vmem_limit_bytes=56 * 2**20
        ),
    )(owners, pattern, docs).reshape(STEPS, 8, 2 * CHIPS * rows)


def from_root(block, axis, owner):
    block = jnp.where(lax.axis_index(axis) == owner, block, jnp.zeros_like(block))
    return lax.psum(block, axis)


def on_device(docs, pattern, owners):
    n_shard = lax.axis_size("shard")
    n_rep = lax.axis_size("rep")
    shard_index = lax.axis_index("shard")
    rep_index = lax.axis_index("rep")
    doc_rows, term_cols = docs.shape
    tile_edge = 128
    row_share = QUERY // (n_shard * n_rep)
    weights = pattern.astype(jnp.bfloat16)
    masked = (
        docs.reshape(doc_rows // tile_edge, tile_edge, term_cols // tile_edge, tile_edge)
        * weights[:, None, :, None]
    ).reshape(doc_rows, term_cols)
    partial_sq = jnp.einsum("dt,dt->d", masked, masked, preferred_element_type=jnp.float32)
    doc_sq = lax.psum(partial_sq, "rep")
    inverse = lax.rsqrt(doc_sq + EPSILON)
    all_inverse = lax.all_gather(inverse, "shard", axis=0, tiled=True)
    sharpen = math.sqrt(TERMS) * 0.5
    results = []
    for step_index in range(STEPS):
        offset = step_index % (doc_rows // QUERY) * QUERY
        candidate = masked[offset : offset + QUERY]
        queries = from_root(candidate, "shard", owners[step_index])
        offset = step_index % (doc_rows // QUERY) * QUERY
        first_global = owners[step_index] * doc_rows + offset
        query_inv = lax.dynamic_slice_in_dim(all_inverse, first_global, QUERY, 0).reshape(
            n_shard, n_rep, row_share
        )
        similar = lax.dot_general(
            queries, masked, (((1,), (1,)), ((), ())), preferred_element_type=jnp.float32
        )
        summed = lax.psum(similar, "rep").reshape(n_shard, n_rep, row_share, doc_rows)
        own_rows = lax.dynamic_index_in_dim(summed, rep_index, 1, keepdims=False)
        received = lax.all_to_all(own_rows, "shard", split_axis=0, concat_axis=2, tiled=True)[0]
        shard_inv = lax.dynamic_index_in_dim(query_inv, shard_index, 0, keepdims=False)
        row_inv = lax.dynamic_index_in_dim(shard_inv, rep_index, 0, keepdims=False)
        scaled = received * row_inv[:, None] * all_inverse[None, :] * sharpen
        results.append(jnp.clip(scaled, -CLIP_LEVEL, CLIP_LEVEL).astype(jnp.bfloat16))
    return jnp.stack(results)


def solution(mesh):
    fits = mesh.shape["shard"] == 2 * CHIPS and mesh.shape["rep"] == REPS
    return jax.shard_map(
        on_ring if fits else on_device,
        mesh=mesh,
        in_specs=(P("shard", "rep"), P("shard", "rep"), P()),
        out_specs=P(None, ("shard", "rep"), None),
        check_vma=False,
    )
```

```python
import math

import jax
import jax.numpy as jnp
from jax import lax
from jax.experimental import pallas as pl
from jax.experimental.pallas import tpu as pltpu
from jax.sharding import PartitionSpec as P

TERMS = 16384
QUERY = 256
STEPS = 4
EDGE = 128


EPSILON = 1e-06
CLIP_LEVEL = 1.5
SHARPEN = math.sqrt(TERMS) * 0.5

CHIPS = 4
REPS = 4
CHUNK = 256
GROUPS = ((0, 1), (2, 3))
STARTS = (0, 3, 6, 9)
LAG = 2
PIECES = 4
MESH = pl.DeviceIdType.MESH


def ring(index):
    return index + (index // 2) * (1 - 2 * (index % 2))


def joined(
    owners, pattern, docs, out,
    mine, cross, stage, arrived, partial, sibling, summed, near, merged, far, norm_parts, inverse, query_column, held, final, landed,
    cross_send, cross_recv, ring_send, ring_recv, core_send, core_recv, rep_send, rep_recv,
    norm_send, norm_recv, inv_send, inv_recv, out_send, out_recv,
):
    shard = lax.axis_index("shard")
    rep = lax.axis_index("rep")
    core = shard % 2
    chip = shard // 2
    place = ring(chip)
    mate = chip * 2 + 1 - core
    onward = ring((place + 1 + 2 * core) % CHIPS) * 2 + core
    chunks = mine.shape[0]
    rows = docs.shape[0]
    shards = 2 * CHIPS

    barrier = pltpu.get_barrier_semaphore()
    for d in range(1, shards):
        pl.semaphore_signal(barrier, inc=1, device_id=((shard + d) % shards, rep), device_id_type=MESH)
    for d in range(1, REPS):
        pl.semaphore_signal(barrier, inc=1, device_id=(shard, (rep + d) % REPS), device_id_type=MESH)
    pl.semaphore_wait(barrier, shards - 1 + REPS - 1)

    def copy(src, dst, send, recv, to):
        return pltpu.make_async_remote_copy(
            src_ref=src, dst_ref=dst, send_sem=send, recv_sem=recv, device_id=to, device_id_type=MESH
        )

    def cross_copy(k):
        return copy(cross.at[k], mine.at[k, core], cross_send.at[k], cross_recv.at[k], (mate, rep))

    def masked_chunk(half, k):
        index = half * chunks + k
        parts = []
        for i in range(rows // EDGE):
            cols = []
            for j in range(CHUNK // EDGE):
                weight = pattern[i, index * (CHUNK // EDGE) + j].astype(jnp.float32)
                block = docs[i * EDGE : (i + 1) * EDGE, pl.ds(pl.multiple_of(index * CHUNK + j * EDGE, EDGE), EDGE)]
                cols.append(block * jnp.full((EDGE, EDGE), weight, jnp.float32).astype(jnp.bfloat16))
            parts.append(cols)
        return parts

    def put(ref, k, lead, parts, squares):
        added = []
        for i, cols in enumerate(parts):
            total = None
            for j, block in enumerate(cols):
                at = (slice(i * EDGE, (i + 1) * EDGE), slice(j * EDGE, (j + 1) * EDGE))
                ref[(k, *lead, *at)] = block
                wide = block.astype(jnp.float32)
                total = wide * wide if total is None else total + wide * wide
            added.append(total)
        return squares + jnp.concatenate(added, axis=0)

    def to_mate(k, squares):
        squares = put(cross, k, (), masked_chunk(1 - core, k), squares)
        cross_copy(k).start()
        return squares

    def to_self(k, squares):
        return put(mine, k, (core,), masked_chunk(core, k), squares)

    squares = lax.fori_loop(0, chunks, to_mate, jnp.zeros((rows, EDGE), jnp.float32))
    squares = lax.fori_loop(0, chunks, to_self, squares)

    def as_row(column):
        return jnp.transpose(jnp.broadcast_to(column, (column.shape[0], 128)))[:8]

    norm_parts[0] = as_row(jnp.sum(squares, axis=1, keepdims=True))

    def norm_copy(d):
        return copy(norm_parts.at[0], norm_parts.at[d], norm_send.at[d], norm_recv.at[d], (shard, (rep + d) % REPS))

    for d in range(1, REPS):
        norm_copy(d).start()

    def inv_copy(d):
        return copy(
            inverse.at[shard], inverse.at[shard], inv_send.at[d], inv_recv.at[d], ((shard + d) % shards, rep)
        )

    def inv_arrival(d):
        slot = inverse.at[(shard + shards - d) % shards]
        return copy(slot, slot, inv_send.at[d], inv_recv.at[d], ((shard + d) % shards, rep))

    def norms():
        for d in range(1, REPS):
            norm_copy(d).wait_recv()
        inverse[shard] = lax.rsqrt(norm_parts[0] + norm_parts[1] + norm_parts[2] + norm_parts[3] + EPSILON)
        for d in range(1, shards):
            inv_copy(d).start()

    def ring_copy(s, t, p):
        lines = pl.ds(p * (QUERY // PIECES), QUERY // PIECES)
        return copy(
            stage.at[s, t, lines], arrived.at[s, t, lines], ring_send.at[s, t, p], ring_recv.at[s, t, p], (onward, rep)
        )

    def core_copy(s):
        return copy(partial.at[s, :, 1 - core], sibling.at[s], core_send.at[s], core_recv.at[s], (mate, rep))

    high, low = rep // 2, rep % 2

    def near_copy(s):
        to = high * 2 + 1 - low
        return copy(summed.at[s, :, :, 1 - low], near.at[s], rep_send.at[s, 0], rep_recv.at[s, 0], (shard, to))

    def far_copy(s):
        to = (1 - high) * 2 + low
        return copy(merged.at[s, :, 1 - high], far.at[s], rep_send.at[s, 1], rep_recv.at[s, 1], (shard, to))

    def out_copy(g, d):
        to = (chip + d) % CHIPS
        lines = pl.ds(g * 16, 16)
        return copy(
            final.at[to, lines], landed.at[chip, lines], out_send.at[g, d - 1], out_recv.at[g, d - 1],
            (to * 2 + core, rep),
        )

    def out_arrival(g, d):
        lines = pl.ds(g * 16, 16)
        slot = landed.at[(chip + CHIPS - d) % CHIPS, lines]
        return copy(slot, slot, out_send.at[g, d - 1], out_recv.at[g, d - 1], (((chip + d) % CHIPS) * 2 + core, rep))

    def to_near(s):
        core_copy(s).wait_recv()
        summed[s] = partial[s, :, core] + sibling[s]
        near_copy(s).start()

    def to_far(s):
        near_copy(s).wait_recv()
        merged[s] = summed[s, :, :, low] + near[s]
        far_copy(s).start()

    def finish(g):
        columns = jnp.concatenate([inverse[2 * chip, 0:1, :], inverse[2 * chip + 1, 0:1, :]], axis=1)
        for s in GROUPS[g]:
            offset = s % (rows // QUERY) * QUERY
            line = inverse[owners[s], 0:1, offset : offset + QUERY]
            query_column[...] = jnp.transpose(jnp.broadcast_to(line, (128, QUERY)))
            far_copy(s).wait_recv()
            for to in range(CHIPS):
                first = pl.multiple_of((to * 2 + core) * 32 + rep * 8, 8)
                total = merged[s, to, high] + far[s, to]
                query_inv = query_column[pl.ds(first, 8), 0:1]
                scaled = total * query_inv * columns * SHARPEN
                held[s % 2, to] = jnp.clip(scaled, -CLIP_LEVEL, CLIP_LEVEL)
        for to in range(CHIPS):
            final[to, g * 16 : (g + 1) * 16, :] = jnp.concatenate([held[0, to], held[1, to]], axis=0).astype(jnp.bfloat16)
        for d in range(1, CHIPS):
            out_copy(g, d).start()

    for s in range(STEPS):
        partial[s] = jnp.zeros(partial.shape[1:], jnp.float32)

    def forward(s, t, p):
        here = jnp.clip(t, 0, chunks - 1)
        lines = slice(p * (QUERY // PIECES), (p + 1) * (QUERY // PIECES))
        first = s % (rows // QUERY) * QUERY + lines.start
        both = [mine[here, c, first : first + QUERY // PIECES, :] for c in range(2)]
        own = jnp.where(owners[s] % 2 == 0, both[0], both[1])
        own = jnp.where(t < chunks, own, jnp.zeros_like(own))
        is_own = owners[s] // 2 == chip

        @pl.when(t == 0)
        def _():
            stage[s, t, lines] = jnp.where(is_own, own, jnp.zeros_like(own))

        @pl.when(t > 0)
        def _():
            ring_copy(s, t - 1, p).wait_recv()
            stage[s, t, lines] = jnp.where(is_own, own, arrived[s, t - 1, lines])

        @pl.when(t < chunks + 2)
        def _():
            ring_copy(s, t, p).start()

    def multiply(s, t):
        away = place + CHIPS - ring(owners[s] // 2)
        away = jnp.where(core == 0, away, 2 * CHIPS - away) % CHIPS
        index = jnp.clip(t - away, 0, chunks - 1)
        block = mine[index].reshape(2 * rows, CHUNK)
        product = lax.dot_general(
            stage[s, t], block, (((1,), (1,)), ((), ())), preferred_element_type=jnp.float32
        )
        partial[s] += product.reshape(partial.shape[1:])

    ends = [start + chunks + 3 for start in STARTS]
    sums = [end + 1 for end in ends]
    halves = [end + 3 for end in ends]
    scored = [max(halves[s] for s in steps) + LAG for steps in GROUPS]
    slots = max(ends)

    for k in range(chunks):
        cross_copy(k).wait_recv()

    def slot(now, carry):
        for p in range(PIECES):
            for s in range(STEPS):
                @pl.when((now >= STARTS[s]) & (now < ends[s]))
                def _(s=s, p=p):
                    forward(s, now - STARTS[s], p)

        @pl.when(now == 2)
        def _():
            norms()

        for s in range(STEPS):
            if sums[s] < slots:
                @pl.when(now == sums[s])
                def _(s=s):
                    to_near(s)

            if halves[s] < slots:
                @pl.when(now == halves[s])
                def _(s=s):
                    to_far(s)

        @pl.when(now == 6)
        def _():
            for d in range(1, shards):
                inv_arrival(d).wait_recv()

        for g in range(len(GROUPS)):
            if scored[g] < slots:
                @pl.when(now == scored[g])
                def _(g=g):
                    finish(g)

        for s in range(STEPS):
            t = now - STARTS[s]

            @pl.when((t >= 0) & (now < ends[s]))
            def _(s=s, t=t):
                multiply(s, t)

            @pl.when(now == ends[s] - 1)
            def _(s=s):
                core_copy(s).start()

        return carry

    lax.fori_loop(0, slots, slot, 0)
    for s in range(STEPS):
        if sums[s] >= slots:
            to_near(s)
    for s in range(STEPS):
        if halves[s] >= slots:
            to_far(s)
    for g in range(len(GROUPS)):
        if scored[g] >= slots:
            finish(g)
    for g in range(len(GROUPS)):
        landed[chip, g * 16 : (g + 1) * 16, :] = final[chip, g * 16 : (g + 1) * 16, :]
    for g in range(len(GROUPS)):
        for d in range(1, CHIPS):
            out_arrival(g, d).wait_recv()
    for c in range(CHIPS):
        out[:, c * 2 * rows : (c + 1) * 2 * rows] = landed[c]

    for k in range(chunks):
        cross_copy(k).wait_send()
    for d in range(1, REPS):
        norm_copy(d).wait_send()
    for d in range(1, shards):
        inv_copy(d).wait_send()
    for s in range(STEPS):
        for p in range(PIECES):
            lax.fori_loop(0, chunks + 2, lambda t, c, s=s, p=p: (ring_copy(s, t, p).wait_send(), c)[1], 0)
        core_copy(s).wait_send()
        near_copy(s).wait_send()
        far_copy(s).wait_send()
    for g in range(len(GROUPS)):
        for d in range(1, CHIPS):
            out_copy(g, d).wait_send()


def on_ring(docs, pattern, owners):
    rows, terms = docs.shape
    chunks = terms // 2 // CHUNK
    bf16, f32 = jnp.bfloat16, jnp.float32
    dma = pltpu.SemaphoreType.DMA
    slots = chunks + 2
    lines = STEPS * 8
    buffers = [
        pltpu.VMEM((chunks, 2, rows, CHUNK), bf16),
        pltpu.VMEM((chunks, rows, CHUNK), bf16),
        pltpu.VMEM((STEPS, slots + 1, QUERY, CHUNK), bf16),
        pltpu.VMEM((STEPS, slots, QUERY, CHUNK), bf16),
        pltpu.VMEM((STEPS, CHIPS, 2, 2, 2, 8, 2 * rows), f32),
        pltpu.VMEM((STEPS, CHIPS, 2, 2, 8, 2 * rows), f32),
        pltpu.VMEM((STEPS, CHIPS, 2, 2, 8, 2 * rows), f32),
        pltpu.VMEM((STEPS, CHIPS, 2, 8, 2 * rows), f32),
        pltpu.VMEM((STEPS, CHIPS, 2, 8, 2 * rows), f32),
        pltpu.VMEM((STEPS, CHIPS, 8, 2 * rows), f32),
        pltpu.VMEM((REPS, 8, rows), f32),
        pltpu.VMEM((2 * CHIPS, 8, rows), f32),
        pltpu.VMEM((QUERY, 128), f32),
        pltpu.VMEM((2, CHIPS, 8, 2 * rows), f32),
        pltpu.VMEM((CHIPS, lines, 2 * rows), bf16),
        pltpu.VMEM((CHIPS, lines, 2 * rows), bf16),
    ]
    semaphores = []
    for shape in (
        (chunks,), (STEPS, slots, PIECES), (STEPS,), (STEPS, 2), (REPS,), (2 * CHIPS,), (len(GROUPS), CHIPS - 1)
    ):
        semaphores += [dma(shape), dma(shape)]
    flops = 2 * STEPS * QUERY * rows * terms
    return pl.pallas_call(
        joined,
        out_shape=jax.ShapeDtypeStruct((lines, 2 * CHIPS * rows), bf16),
        in_specs=[
            pl.BlockSpec(memory_space=pltpu.SMEM),
            pl.BlockSpec(memory_space=pltpu.SMEM),
            pl.BlockSpec(memory_space=pltpu.VMEM),
        ],
        out_specs=pl.BlockSpec(memory_space=pltpu.VMEM),
        scratch_shapes=buffers + semaphores,
        cost_estimate=pl.CostEstimate(flops=flops, bytes_accessed=rows * terms * 2, transcendentals=0),
        compiler_params=pltpu.CompilerParams(
            collective_id=0, has_side_effects=True, vmem_limit_bytes=56 * 2**20
        ),
    )(owners, pattern, docs).reshape(STEPS, 8, 2 * CHIPS * rows)


def from_root(block, axis, owner):
    block = jnp.where(lax.axis_index(axis) == owner, block, jnp.zeros_like(block))
    return lax.psum(block, axis)


def on_device(docs, pattern, owners):
    n_shard = lax.axis_size("shard")
    n_rep = lax.axis_size("rep")
    shard_index = lax.axis_index("shard")
    rep_index = lax.axis_index("rep")
    doc_rows, term_cols = docs.shape
    tile_edge = 128
    row_share = QUERY // (n_shard * n_rep)
    weights = pattern.astype(jnp.bfloat16)
    masked = (
        docs.reshape(doc_rows // tile_edge, tile_edge, term_cols // tile_edge, tile_edge)
        * weights[:, None, :, None]
    ).reshape(doc_rows, term_cols)
    partial_sq = jnp.einsum("dt,dt->d", masked, masked, preferred_element_type=jnp.float32)
    doc_sq = lax.psum(partial_sq, "rep")
    inverse = lax.rsqrt(doc_sq + EPSILON)
    all_inverse = lax.all_gather(inverse, "shard", axis=0, tiled=True)
    sharpen = math.sqrt(TERMS) * 0.5
    results = []
    for step_index in range(STEPS):
        offset = step_index % (doc_rows // QUERY) * QUERY
        candidate = masked[offset : offset + QUERY]
        queries = from_root(candidate, "shard", owners[step_index])
        offset = step_index % (doc_rows // QUERY) * QUERY
        first_global = owners[step_index] * doc_rows + offset
        query_inv = lax.dynamic_slice_in_dim(all_inverse, first_global, QUERY, 0).reshape(
            n_shard, n_rep, row_share
        )
        similar = lax.dot_general(
            queries, masked, (((1,), (1,)), ((), ())), preferred_element_type=jnp.float32
        )
        summed = lax.psum(similar, "rep").reshape(n_shard, n_rep, row_share, doc_rows)
        own_rows = lax.dynamic_index_in_dim(summed, rep_index, 1, keepdims=False)
        received = lax.all_to_all(own_rows, "shard", split_axis=0, concat_axis=2, tiled=True)[0]
        shard_inv = lax.dynamic_index_in_dim(query_inv, shard_index, 0, keepdims=False)
        row_inv = lax.dynamic_index_in_dim(shard_inv, rep_index, 0, keepdims=False)
        scaled = received * row_inv[:, None] * all_inverse[None, :] * sharpen
        results.append(jnp.clip(scaled, -CLIP_LEVEL, CLIP_LEVEL).astype(jnp.bfloat16))
    return jnp.stack(results)


def solution(mesh):
    fits = mesh.shape["shard"] == 2 * CHIPS and mesh.shape["rep"] == REPS
    return jax.shard_map(
        on_ring if fits else on_device,
        mesh=mesh,
        in_specs=(P("shard", "rep"), P("shard", "rep"), P()),
        out_specs=P(None, ("shard", "rep"), None),
        check_vma=False,
    )
```
